32 devices in a mesh: dp: 16 (over z, x, core), tensor: 2 (over y).
Axes of the slice: x: 2, y: 2, z: 4, core: 2. Of those that a mesh axis runs over, the one named last changes fastest.
Arguments:
- tokens: bfloat16 [8192, 8192], P('dp', 'tensor'), may hold values from -6 to 6
- cotangent: bfloat16 [8192, 1024], P('dp', 'tensor'), may hold values from -6 to 6
- frozen_key_weight: bfloat16 [8192, 1024], P(None, 'tensor'), may hold values from -0.0625 to 0.0625
- counts: int32 [16, 16], P('dp'), may hold values from 1 to 48, 512 in all within a row
- holder_assignment: int32 [16], replicated, may hold values from 0 to 15, each once
- adapter_down_matrix: float32 [16, 64, 8192], P('dp', None, 'tensor'), may hold values from -0.0625 to 0.0625
- adapter_up_matrix: float32 [16, 64, 1024], P('dp', None, 'tensor'), may hold values from -0.06 to 0.06
- down_first_moment: float32 [16, 64, 8192], P('dp', None, 'tensor'), may hold values from -12 to 12
- down_second_moment: float32 [16, 64, 8192], P('dp', None, 'tensor'), may hold values from 1 to 100
- up_first_moment: float32 [16, 64, 1024], P('dp', None, 'tensor'), may hold values from -30 to 30
- up_second_moment: float32 [16, 64, 1024], P('dp', None, 'tensor'), may hold values from 10 to 1000
Outputs:
- layer_out: bfloat16 [8192, 1024], P('dp', 'tensor')
- input_grad: bfloat16 [8192, 8192], P('dp', 'tensor')
- fresh_down_matrix: float32 [16, 64, 8192], P('dp', None, 'tensor')
- fresh_down_first: float32 [16, 64, 8192], P('dp', None, 'tensor')
- fresh_down_second: float32 [16, 64, 8192], P('dp', None, 'tensor')
- fresh_up_matrix: float32 [16, 64, 1024], P('dp', None, 'tensor')
- fresh_up_first: float32 [16, 64, 1024], P('dp', None, 'tensor')
- fresh_up_second: float32 [16, 64, 1024], P('dp', None, 'tensor')
The draws below stay inside these ranges and needn't reach their ends.
Inputs may be any that keep to these rules, and one draw needn't show every extreme that they name: `counts`: row j gives, adapter by adapter in order, how many of dp index j's tokens belong to each adapter; dp index j's rows of tokens and cotangent are grouped in that order; each row sums to 512, and some entry of each row equals 48. A permutation: holder_assignment[a] is the dp index that holds adapter a.
All inputs are finite; a program needn't handle non-finite values.
Results may differ from the reference program's by a relative error of at most 0.0021.
Values may be sent and summed in bfloat16 or wider, within the bound.
A program may use at most 128 MiB of HBM per device.

```python
import math
import jax
import jax.numpy as jnp
import numpy as np
from jax import lax

MODEL_WIDTH = 8192
KEY_OUTPUTS = 1024
ADAPTER_RANK = 64
TOK_DEV = 512
ADAPTER_COUNT = 16
CAP = 48
TOKENS = 8192
N_DP = 16


def shard_levels(rng, dims, shards, least, largest):
    def one(position, blocks):
        draws = jax.random.uniform(jax.random.fold_in(jax.random.fold_in(rng, 6), position), (blocks,), jnp.float32, least / len(shards), largest / len(shards))
        return jnp.repeat(jnp.exp(draws), dims[position] // blocks).reshape((-1,) + (1,) * (len(dims) - position - 1))

    gain = one(*shards[0])
    for cut in shards[1:]:
        gain = gain * one(*cut)
    return gain


def length_profile(count, total, most, lean):
    weights = [(1 << 20) // math.isqrt(grade ** lean) + 1 for grade in range(2, count + 1)]
    spare, given = total - most - (count - 1), [1] * (count - 1)
    while spare > 0:
        movable = [i for i in range(count - 1) if given[i] < most]
        whole, budget = sum([weights[i] for i in movable]), spare
        for i in movable:
            addition = min(most - given[i], max(1, budget * weights[i] // whole), spare)
            given[i] = given[i] + addition
            spare = spare - addition
    return np.array([most] + given)


def uneven(stream_key, amount, total, reach, skew):
    if amount == 2:
        one = jax.random.randint(stream_key, (), max(1, total - reach), min(reach, total - 1) + 1)
        return jnp.stack([one, total - one])
    tallies = jnp.asarray(length_profile(amount, total, reach, skew), jnp.int32)
    twos = (amount - 1) // 2
    donor, receiver = tallies[1:1 + 2 * twos:2], tallies[2:2 + 2 * twos:2]
    margin = jnp.minimum(donor - 1, reach - receiver)
    passed = jax.random.randint(jax.random.fold_in(stream_key, 1), (twos,), 0, 1 << 20) % (margin + 1)
    tallies = tallies.at[1:1 + 2 * twos:2].set(donor - passed).at[2:2 + 2 * twos:2].set(receiver + passed)
    return tallies[jax.random.permutation(jax.random.fold_in(stream_key, 2), amount)]


def scatter_about(key, shape, scale, bound, shards=(), held_as=jnp.bfloat16):
    drawn = scale * jax.random.normal(key, shape, jnp.float32)
    if shards:
        drawn = drawn * shard_levels(key, shape, shards, -0.22, 0.18)
    return jnp.clip(drawn, -bound, bound).astype(held_as)


def setup_inputs(seed: int = 0) -> dict:
    keys = jax.random.split(jax.random.key(seed), 12)
    tokens = scatter_about(keys[0], (TOKENS, MODEL_WIDTH), 1.0, 6.0, ((0, 16), (1, 2)))
    cotangent = scatter_about(keys[1], (TOKENS, KEY_OUTPUTS), 1.0, 6.0, ((0, 16), (1, 2)))
    frozen_key_weight = scatter_about(keys[2], (MODEL_WIDTH, KEY_OUTPUTS), MODEL_WIDTH ** -0.5, 0.0625, ((1, 2),))
    counts = jax.vmap(lambda own: uneven(own, ADAPTER_COUNT, TOK_DEV, CAP, 2))(jax.random.split(keys[3], N_DP)).reshape((N_DP, ADAPTER_COUNT)).astype(jnp.int32)
    holder_assignment = jax.random.permutation(keys[4], ADAPTER_COUNT).astype(jnp.int32)
    adapter_down_matrix = scatter_about(keys[5], (ADAPTER_COUNT, ADAPTER_RANK, MODEL_WIDTH), MODEL_WIDTH ** -0.5, 0.0625, ((0, 16), (2, 2)), jnp.float32)
    adapter_up_matrix = scatter_about(keys[6], (ADAPTER_COUNT, ADAPTER_RANK, KEY_OUTPUTS), 0.01, 0.06, ((0, 16), (2, 2)), jnp.float32)
    down_first_moment = scatter_about(keys[7], (ADAPTER_COUNT, ADAPTER_RANK, MODEL_WIDTH), 2.0, 12.0, ((0, 16), (2, 2)), jnp.float32)
    down_second_moment = jnp.clip(jnp.exp(math.log(100.0) - 4.6051702 * jax.random.uniform(keys[8], (ADAPTER_COUNT, ADAPTER_RANK, MODEL_WIDTH), jnp.float32) ** shard_levels(keys[8], (ADAPTER_COUNT, ADAPTER_RANK, MODEL_WIDTH), ((0, 16), (2, 2)), -0.2, 0.2)), 1.0, 100.0)
    up_first_moment = scatter_about(keys[9], (ADAPTER_COUNT, ADAPTER_RANK, KEY_OUTPUTS), 5.0, 30.0, ((0, 16), (2, 2)), jnp.float32)
    up_second_moment = jnp.clip(jnp.exp(math.log(1000.0) - 4.6051702 * jax.random.uniform(keys[10], (ADAPTER_COUNT, ADAPTER_RANK, KEY_OUTPUTS), jnp.float32) ** shard_levels(keys[10], (ADAPTER_COUNT, ADAPTER_RANK, KEY_OUTPUTS), ((0, 16), (2, 2)), -0.2, 0.2)), 10.0, 1000.0)
    return {"tokens": tokens, "cotangent": cotangent, "frozen_key_weight": frozen_key_weight, "counts": counts, "holder_assignment": holder_assignment, "adapter_down_matrix": adapter_down_matrix, "adapter_up_matrix": adapter_up_matrix, "down_first_moment": down_first_moment, "down_second_moment": down_second_moment, "up_first_moment": up_first_moment, "up_second_moment": up_second_moment}


adapter_scale = 2.0
learn_rate = 0.01
beta_one = 0.9
beta_two = 0.999
adam_eps = 1e-08
adam_step = 10

def optimizer_update(weight, moment, second, grad):
    moment_new = beta_one * moment + (1.0 - beta_one) * grad
    second_new = beta_two * second + (1.0 - beta_two) * grad * grad
    first_fix = 1.0 - beta_one ** adam_step
    second_fix = 1.0 - beta_two ** adam_step
    weight_new = weight - learn_rate * (moment_new / first_fix) / (jnp.sqrt(second_new / second_fix) + adam_eps)
    return (weight_new, moment_new, second_new)

def reference(tokens, cotangent, frozen_key_weight, counts, holder_assignment, adapter_down_matrix, adapter_up_matrix, down_first_moment, down_second_moment, up_first_moment, up_second_moment):
    base_out = jnp.dot(tokens, frozen_key_weight, preferred_element_type=jnp.float32)
    base_grad = jnp.dot(cotangent, frozen_key_weight.T, preferred_element_type=jnp.float32)
    upper = jnp.cumsum(counts, axis=1).astype(jnp.int32)
    lower = (upper - counts).astype(jnp.int32)
    adapter_iota = jnp.arange(ADAPTER_COUNT, dtype=jnp.int32)
    inverse = lax.optimization_barrier(jnp.sum(jnp.where(holder_assignment[None, :] == adapter_iota[:, None], adapter_iota[None, :], 0), axis=1)).astype(jnp.int32)
    slot_iota = jnp.arange(CAP, dtype=jnp.int32)
    source_iota = jnp.arange(N_DP, dtype=jnp.int32)

    def owner_step(carry, holder_index):
        extra_out, extra_grad = carry
        adapter = inverse[holder_index]
        start_rows = lower[:, adapter]
        live_count = counts[:, adapter]
        live = slot_iota[None, :] < live_count[:, None]
        index = jnp.where(live, source_iota[:, None] * TOK_DEV + start_rows[:, None] + slot_iota[None, :], 0)
        index = index.reshape(-1).astype(jnp.int32)
        keep = live.reshape(-1)[:, None]
        x_rows = jnp.where(keep, tokens[index], jnp.zeros((), tokens.dtype))
        gradient_rows = jnp.where(keep, cotangent[index], jnp.zeros((), cotangent.dtype))
        down_half16 = adapter_down_matrix[holder_index].astype(jnp.bfloat16)
        up_half16 = adapter_up_matrix[holder_index].astype(jnp.bfloat16)
        hidden = jnp.dot(x_rows, down_half16.T, preferred_element_type=jnp.float32)
        hidden_backward = adapter_scale * jnp.dot(gradient_rows, up_half16.T, preferred_element_type=jnp.float32)
        hidden_half16 = hidden.astype(jnp.bfloat16)
        back16 = hidden_backward.astype(jnp.bfloat16)
        adapter_output = (adapter_scale * jnp.dot(hidden_half16, up_half16, preferred_element_type=jnp.float32)).astype(jnp.bfloat16)
        adapter_grad = jnp.dot(back16, down_half16, preferred_element_type=jnp.float32).astype(jnp.bfloat16)
        down_gradient = jnp.dot(back16.T, x_rows, preferred_element_type=jnp.float32)
        up_gradient = adapter_scale * jnp.dot(hidden_half16.T, gradient_rows, preferred_element_type=jnp.float32)
        extra_out = extra_out.at[index].add(jnp.where(keep, adapter_output, jnp.zeros((), adapter_output.dtype)))
        extra_grad = extra_grad.at[index].add(jnp.where(keep, adapter_grad, jnp.zeros((), adapter_grad.dtype)))
        return ((extra_out, extra_grad), (down_gradient, up_gradient))
    start_carry = (jnp.zeros((TOKENS, KEY_OUTPUTS), jnp.bfloat16), jnp.zeros((TOKENS, MODEL_WIDTH), jnp.bfloat16))
    (extra_out, extra_grad), (down_gradient, up_gradient) = lax.scan(owner_step, start_carry, adapter_iota)
    layer_out = (base_out + extra_out.astype(jnp.float32)).astype(jnp.bfloat16)
    input_grad = (base_grad + extra_grad.astype(jnp.float32)).astype(jnp.bfloat16)
    fresh_down_matrix, fresh_down_first, fresh_down_second = optimizer_update(adapter_down_matrix, down_first_moment, down_second_moment, down_gradient)
    fresh_up_matrix, fresh_up_first, fresh_up_second = optimizer_update(adapter_up_matrix, up_first_moment, up_second_moment, up_gradient)
    return (layer_out, input_grad, fresh_down_matrix, fresh_down_first, fresh_down_second, fresh_up_matrix, fresh_up_first, fresh_up_second)
```

```python
import jax
import jax.numpy as jnp
from jax import lax
from jax.sharding import PartitionSpec as P

adapter_scale = 2.0
learn_rate = 0.01
beta_one = 0.9
beta_two = 0.999
adam_eps = 1e-08
adam_step = 10


def optimizer_update(weight, moment, second, grad):
    moment_new = beta_one * moment + (1.0 - beta_one) * grad
    second_new = beta_two * second + (1.0 - beta_two) * grad * grad
    first_fix = 1.0 - beta_one**adam_step
    second_fix = 1.0 - beta_two**adam_step
    weight_new = weight - learn_rate * (moment_new / first_fix) / (
        jnp.sqrt(second_new / second_fix) + adam_eps
    )
    return (weight_new, moment_new, second_new)


def owner_mask(counts_row, holders, rows, rank):
    n_owner = holders.shape[0]
    order = jnp.arange(n_owner, dtype=jnp.int32)
    upper = jnp.sum(jnp.where(order[None, :] <= order[:, None], counts_row[None, :], 0), axis=1)
    lower = upper - counts_row
    select = holders[None, :] == jnp.arange(n_owner, dtype=jnp.int32)[:, None]
    start = jnp.sum(jnp.where(select, lower[None, :], 0), axis=1)
    stop = jnp.sum(jnp.where(select, upper[None, :], 0), axis=1)
    start = jnp.repeat(start, rank)
    stop = jnp.repeat(stop, rank)
    token = jnp.arange(rows, dtype=jnp.int32)[:, None]
    return (token >= start[None, :]) & (token < stop[None, :])


def fold(masked, width):
    total = masked[:, :width]
    for k in range(1, masked.shape[1] // width):
        total = total + masked[:, k * width : (k + 1) * width]
    return total


def dot(a, b, contract):
    return lax.dot_general(a, b, (contract, ((), ())), preferred_element_type=jnp.float32)


def make(n_dp, n_tensor):
    def ring(shift):
        return [(i, (i + shift) % n_tensor) for i in range(n_tensor)]

    swap_core = [(i, i ^ 1) for i in range(n_dp)]

    def per_device(
        tokens,
        cotangent,
        frozen_key_weight,
        counts,
        holder_assignment,
        adapter_down_matrix,
        adapter_up_matrix,
        down_first_moment,
        down_second_moment,
        up_first_moment,
        up_second_moment,
    ):
        rows, feat = tokens.shape
        keys = cotangent.shape[1]
        rank = adapter_down_matrix.shape[1]
        n_owner = holder_assignment.shape[0]
        width = 2 * rank
        half = feat // 2
        mine = lax.axis_index("tensor")
        core = lax.axis_index("dp") % 2
        bf = jnp.bfloat16

        both16 = jnp.concatenate(
            [adapter_down_matrix[0].astype(bf), adapter_up_matrix[0].astype(bf)], axis=1
        )
        all16 = lax.all_gather(both16, "dp", axis=0, tiled=True)

        weight_mine = lax.dynamic_slice_in_dim(frozen_key_weight, mine * feat, feat, 0)
        cots, weights = [cotangent], [weight_mine]
        for shift in range(1, n_tensor):
            cots.append(lax.ppermute(cotangent, "tensor", ring(shift)))
            target = lax.rem(mine + shift, n_tensor)
            got = lax.ppermute(
                lax.dynamic_slice_in_dim(frozen_key_weight, target * feat + core * half, half, 0),
                "tensor",
                ring(shift),
            )
            got_peer = lax.ppermute(got, "dp", swap_core)
            weights.append(
                jnp.concatenate(
                    [jnp.where(core == 0, got, got_peer), jnp.where(core == 0, got_peer, got)],
                    axis=0,
                )
            )

        base_out = dot(tokens, weight_mine, ((1,), (0,)))
        for shift in range(1, n_tensor):
            base_out = base_out + lax.ppermute(
                dot(tokens, weights[shift], ((1,), (0,))), "tensor", ring(-shift)
            )

        mask = owner_mask(counts[0], holder_assignment, rows, rank)
        down_all = all16[:, :feat]
        up_all = all16[:, feat:]
        hidden_part = fold(jnp.where(mask, dot(tokens, down_all, ((1,), (1,))), 0.0), width)
        back_part = fold(jnp.where(mask, dot(cotangent, up_all, ((1,), (1,))), 0.0), width)
        part = jnp.concatenate([hidden_part, adapter_scale * back_part], axis=1)
        summed = part
        for shift in range(1, n_tensor):
            summed = summed + lax.ppermute(part, "tensor", ring(shift))
        times = n_owner * rank // width
        zero = jnp.zeros((), bf)
        hidden16 = jnp.where(mask, jnp.tile(summed[:, :width].astype(bf), (1, times)), zero)
        back16 = jnp.where(mask, jnp.tile(summed[:, width:].astype(bf), (1, times)), zero)

        down_part = dot(back16, tokens, ((0,), (0,)))
        up_part = adapter_scale * dot(hidden16, cotangent, ((0,), (0,)))
        down_gradient = lax.psum_scatter(down_part, "dp", scatter_dimension=0, tiled=True)
        up_gradient = lax.psum_scatter(up_part, "dp", scatter_dimension=0, tiled=True)

        layer_out = (
            base_out + adapter_scale * dot(hidden16, up_all, ((1,), (0,)))
        ).astype(bf)
        base_grad = dot(back16, down_all, ((1,), (0,)))
        for cot, weight in zip(cots, weights):
            base_grad = base_grad + dot(cot, weight, ((1,), (1,)))
        input_grad = base_grad.astype(bf)
        fresh_down = optimizer_update(
            adapter_down_matrix[0], down_first_moment[0], down_second_moment[0], down_gradient
        )
        fresh_up = optimizer_update(
            adapter_up_matrix[0], up_first_moment[0], up_second_moment[0], up_gradient
        )
        return (layer_out, input_grad) + tuple(x[None] for x in fresh_down + fresh_up)

    return per_device


def solution(mesh):
    placed = (
        P("dp", "tensor"),
        P("dp", "tensor"),
        P(None, "tensor"),
        P("dp", None),
        P(),
        P("dp", None, "tensor"),
        P("dp", None, "tensor"),
        P("dp", None, "tensor"),
        P("dp", None, "tensor"),
        P("dp", None, "tensor"),
        P("dp", None, "tensor"),
    )
    return jax.shard_map(
        make(mesh.shape["dp"], mesh.shape["tensor"]),
        mesh=mesh,
        in_specs=placed,
        out_specs=(
            P("dp", "tensor"),
            P("dp", "tensor"),
            P("dp", None, "tensor"),
            P("dp", None, "tensor"),
            P("dp", None, "tensor"),
            P("dp", None, "tensor"),
            P("dp", None, "tensor"),
            P("dp", None, "tensor"),
        ),
        check_vma=False,
    )
```

```python
import jax
import jax.numpy as jnp
from jax import lax
from jax.sharding import PartitionSpec as P

adapter_scale = 2.0
learn_rate = 0.01
beta_one = 0.9
beta_two = 0.999
adam_eps = 1e-08
adam_step = 10


def optimizer_update(weight, moment, second, grad):
    moment_new = beta_one * moment + (1.0 - beta_one) * grad
    second_new = beta_two * second + (1.0 - beta_two) * grad * grad
    first_fix = 1.0 - beta_one**adam_step
    second_fix = 1.0 - beta_two**adam_step
    weight_new = weight - learn_rate * (moment_new / first_fix) / (
        jnp.sqrt(second_new / second_fix) + adam_eps
    )
    return (weight_new, moment_new, second_new)


def owner_masks(counts_row, holders, rows, rank):
    n_owner = holders.shape[0]
    order = jnp.arange(n_owner, dtype=jnp.int32)
    upper = jnp.sum(jnp.where(order[None, :] <= order[:, None], counts_row[None, :], 0), axis=1)
    lower = upper - counts_row
    select = holders[None, :] == jnp.arange(n_owner, dtype=jnp.int32)[:, None]
    start = jnp.sum(jnp.where(select, lower[None, :], 0), axis=1)
    stop = jnp.sum(jnp.where(select, upper[None, :], 0), axis=1)
    capacity = 3 * rows // (2 * n_owner)
    token = jnp.arange(rows, dtype=jnp.int32)
    slot_token = (start[:, None] + jnp.arange(capacity, dtype=jnp.int32)[None, :]).reshape(-1)
    slot_stop = jnp.repeat(stop, capacity)
    slots = (token[None, :] == slot_token[:, None]) & (token[None, :] < slot_stop[:, None])
    start = jnp.repeat(start, rank)
    stop = jnp.repeat(stop, rank)
    mask = (token[:, None] >= start[None, :]) & (token[:, None] < stop[None, :])
    return mask, slots


def fold(masked, width):
    total = masked[:, :width]
    for k in range(1, masked.shape[1] // width):
        total = total + masked[:, k * width : (k + 1) * width]
    return total


def dot(a, b, contract):
    return lax.dot_general(a, b, (contract, ((), ())), preferred_element_type=jnp.float32)


def make(n_dp, n_tensor):
    def ring(shift):
        return [(i, (i + shift) % n_tensor) for i in range(n_tensor)]

    swap_core = [(i, i ^ 1) for i in range(n_dp)]

    def per_device(
        tokens,
        cotangent,
        frozen_key_weight,
        counts,
        holder_assignment,
        adapter_down_matrix,
        adapter_up_matrix,
        down_first_moment,
        down_second_moment,
        up_first_moment,
        up_second_moment,
    ):
        rows, feat = tokens.shape
        keys = cotangent.shape[1]
        rank = adapter_down_matrix.shape[1]
        n_owner = holder_assignment.shape[0]
        width = 2 * rank
        half = feat // 2
        mine = lax.axis_index("tensor")
        core = lax.axis_index("dp") % 2
        bf = jnp.bfloat16

        mask, slots = owner_masks(counts[0], holder_assignment, rows, rank)
        pick = slots.astype(bf)
        send = jnp.concatenate(
            [dot(pick, x, ((1,), (0,))).astype(bf) for x in (tokens, cotangent)], axis=1
        )
        routed = lax.all_to_all(
            send.reshape(n_owner, -1, feat + keys), "dp", split_axis=0, concat_axis=0, tiled=True
        ).reshape(-1, feat + keys)
        both16 = jnp.concatenate(
            [adapter_down_matrix[0].astype(bf), adapter_up_matrix[0].astype(bf)], axis=1
        )
        all16 = lax.all_gather(both16, "dp", axis=0, tiled=True)

        weight_mine = lax.dynamic_slice_in_dim(frozen_key_weight, mine * feat, feat, 0)
        cots, weights = [cotangent], [weight_mine]
        for shift in range(1, n_tensor):
            cots.append(lax.ppermute(cotangent, "tensor", ring(shift)))
            target = lax.rem(mine + shift, n_tensor)
            got = lax.ppermute(
                lax.dynamic_slice_in_dim(frozen_key_weight, target * feat + core * half, half, 0),
                "tensor",
                ring(shift),
            )
            got_peer = lax.ppermute(got, "dp", swap_core)
            weights.append(
                jnp.concatenate(
                    [jnp.where(core == 0, got, got_peer), jnp.where(core == 0, got_peer, got)],
                    axis=0,
                )
            )

        base_out = dot(tokens, weight_mine, ((1,), (0,)))
        for shift in range(1, n_tensor):
            base_out = base_out + lax.ppermute(
                dot(tokens, weights[shift], ((1,), (0,))), "tensor", ring(-shift)
            )

        down_all = all16[:, :feat]
        up_all = all16[:, feat:]
        hidden_part = fold(jnp.where(mask, dot(tokens, down_all, ((1,), (1,))), 0.0), width)
        back_part = fold(jnp.where(mask, dot(cotangent, up_all, ((1,), (1,))), 0.0), width)
        part = jnp.concatenate([hidden_part, adapter_scale * back_part], axis=1)
        summed = part
        for shift in range(1, n_tensor):
            summed = summed + lax.ppermute(part, "tensor", ring(shift))
        times = n_owner * rank // width
        zero = jnp.zeros((), bf)
        hidden16 = jnp.where(mask, jnp.tile(summed[:, :width].astype(bf), (1, times)), zero)
        back16 = jnp.where(mask, jnp.tile(summed[:, width:].astype(bf), (1, times)), zero)

        x_rows, cot_rows = routed[:, :feat], routed[:, feat:]
        own_part = jnp.concatenate(
            [
                dot(x_rows, both16[:, :feat], ((1,), (1,))),
                adapter_scale * dot(cot_rows, both16[:, feat:], ((1,), (1,))),
            ],
            axis=1,
        )
        own = own_part
        for shift in range(1, n_tensor):
            own = own + lax.ppermute(own_part, "tensor", ring(shift))
        own16 = own.astype(bf)
        down_gradient = dot(own16[:, rank:], x_rows, ((0,), (0,)))
        up_gradient = adapter_scale * dot(own16[:, :rank], cot_rows, ((0,), (0,)))

        layer_out = (
            base_out + adapter_scale * dot(hidden16, up_all, ((1,), (0,)))
        ).astype(bf)
        base_grad = dot(back16, down_all, ((1,), (0,)))
        for cot, weight in zip(cots, weights):
            base_grad = base_grad + dot(cot, weight, ((1,), (1,)))
        input_grad = base_grad.astype(bf)
        fresh_down = optimizer_update(
            adapter_down_matrix[0], down_first_moment[0], down_second_moment[0], down_gradient
        )
        fresh_up = optimizer_update(
            adapter_up_matrix[0], up_first_moment[0], up_second_moment[0], up_gradient
        )
        return (layer_out, input_grad) + tuple(x[None] for x in fresh_down + fresh_up)

    return per_device


def solution(mesh):
    placed = (
        P("dp", "tensor"),
        P("dp", "tensor"),
        P(None, "tensor"),
        P("dp", None),
        P(),
        P("dp", None, "tensor"),
        P("dp", None, "tensor"),
        P("dp", None, "tensor"),
        P("dp", None, "tensor"),
        P("dp", None, "tensor"),
        P("dp", None, "tensor"),
    )
    return jax.shard_map(
        make(mesh.shape["dp"], mesh.shape["tensor"]),
        mesh=mesh,
        in_specs=placed,
        out_specs=(
            P("dp", "tensor"),
            P("dp", "tensor"),
            P("dp", None, "tensor"),
            P("dp", None, "tensor"),
            P("dp", None, "tensor"),
            P("dp", None, "tensor"),
            P("dp", None, "tensor"),
            P("dp", None, "tensor"),
        ),
        check_vma=False,
    )
```

```python
import jax
import jax.numpy as jnp
from jax import lax
from jax.sharding import PartitionSpec as P

adapter_scale = 2.0
learn_rate = 0.01
beta_one = 0.9
beta_two = 0.999
adam_eps = 1e-08
adam_step = 10


def optimizer_update(weight, moment, second, grad):
    moment_new = beta_one * moment + (1.0 - beta_one) * grad
    second_new = beta_two * second + (1.0 - beta_two) * grad * grad
    first_fix = 1.0 - beta_one**adam_step
    second_fix = 1.0 - beta_two**adam_step
    weight_new = weight - learn_rate * (moment_new / first_fix) / (
        jnp.sqrt(second_new / second_fix) + adam_eps
    )
    return (weight_new, moment_new, second_new)


def owner_masks(counts_row, holders, rows, rank):
    n_owner = holders.shape[0]
    order = jnp.arange(n_owner, dtype=jnp.int32)
    upper = jnp.sum(jnp.where(order[None, :] <= order[:, None], counts_row[None, :], 0), axis=1)
    lower = upper - counts_row
    select = holders[None, :] == jnp.arange(n_owner, dtype=jnp.int32)[:, None]
    start = jnp.sum(jnp.where(select, lower[None, :], 0), axis=1)
    stop = jnp.sum(jnp.where(select, upper[None, :], 0), axis=1)
    capacity = 3 * rows // (2 * n_owner)
    token = jnp.arange(rows, dtype=jnp.int32)
    slot_token = (start[:, None] + jnp.arange(capacity, dtype=jnp.int32)[None, :]).reshape(-1)
    slot_stop = jnp.repeat(stop, capacity)
    slots = (token[None, :] == slot_token[:, None]) & (token[None, :] < slot_stop[:, None])
    start = jnp.repeat(start, rank)
    stop = jnp.repeat(stop, rank)
    mask = (token[:, None] >= start[None, :]) & (token[:, None] < stop[None, :])
    return mask, slots


def fold(masked, width):
    total = masked[:, :width]
    for k in range(1, masked.shape[1] // width):
        total = total + masked[:, k * width : (k + 1) * width]
    return total


def dot(a, b, contract):
    return lax.dot_general(a, b, (contract, ((), ())), preferred_element_type=jnp.float32)


def make(n_dp, n_tensor):
    def ring(shift):
        return [(i, (i + shift) % n_tensor) for i in range(n_tensor)]

    swap_core = [(i, i ^ 1) for i in range(n_dp)]

    def per_device(
        tokens,
        cotangent,
        frozen_key_weight,
        counts,
        holder_assignment,
        adapter_down_matrix,
        adapter_up_matrix,
        down_first_moment,
        down_second_moment,
        up_first_moment,
        up_second_moment,
    ):
        rows, feat = tokens.shape
        keys = cotangent.shape[1]
        rank = adapter_down_matrix.shape[1]
        n_owner = holder_assignment.shape[0]
        width = 2 * rank
        half = feat // 2
        mine = lax.axis_index("tensor")
        core = lax.axis_index("dp") % 2
        bf = jnp.bfloat16

        mask, slots = owner_masks(counts[0], holder_assignment, rows, rank)
        pick = slots.astype(bf)
        send = jnp.concatenate(
            [dot(pick, x, ((1,), (0,))).astype(bf) for x in (tokens, cotangent)], axis=1
        )
        routed = lax.all_to_all(
            send.reshape(n_owner, -1, feat + keys), "dp", split_axis=0, concat_axis=0, tiled=True
        ).reshape(-1, feat + keys)
        both16 = jnp.concatenate(
            [adapter_down_matrix[0].astype(bf), adapter_up_matrix[0].astype(bf)], axis=1
        )
        all16 = lax.all_gather(both16, "dp", axis=0, tiled=True)

        weight_mine = lax.dynamic_slice_in_dim(frozen_key_weight, mine * feat, feat, 0)
        cots, weights = [cotangent], [weight_mine]
        for shift in range(1, n_tensor):
            cots.append(lax.ppermute(cotangent, "tensor", ring(shift)))
            target = lax.rem(mine + shift, n_tensor)
            got = lax.ppermute(
                lax.dynamic_slice_in_dim(frozen_key_weight, target * feat + core * half, half, 0),
                "tensor",
                ring(shift),
            )
            got_peer = lax.ppermute(got, "dp", swap_core)
            weights.append(
                jnp.concatenate(
                    [jnp.where(core == 0, got, got_peer), jnp.where(core == 0, got_peer, got)],
                    axis=0,
                )
            )

        base_out = dot(tokens, weight_mine, ((1,), (0,)))
        for shift in range(1, n_tensor):
            base_out = base_out + lax.ppermute(
                dot(tokens, weights[shift], ((1,), (0,))), "tensor", ring(-shift)
            )

        down_all = all16[:, :feat]
        up_all = all16[:, feat:]
        hidden_part = fold(jnp.where(mask, dot(tokens, down_all, ((1,), (1,))), 0.0), width)
        back_part = fold(jnp.where(mask, dot(cotangent, up_all, ((1,), (1,))), 0.0), width)
        part = jnp.concatenate([hidden_part, adapter_scale * back_part], axis=1)
        summed = part
        for shift in range(1, n_tensor):
            summed = summed + lax.ppermute(part, "tensor", ring(shift))
        times = n_owner * rank // width
        zero = jnp.zeros((), bf)
        hidden16 = jnp.where(mask, jnp.tile(summed[:, :width].astype(bf), (1, times)), zero)
        back16 = jnp.where(mask, jnp.tile(summed[:, width:].astype(bf), (1, times)), zero)

        layer_out = (
            base_out + adapter_scale * dot(hidden16, up_all, ((1,), (0,)))
        ).astype(bf)
        base_grad = dot(back16, down_all, ((1,), (0,)))
        for cot, weight in zip(cots, weights):
            base_grad = base_grad + dot(cot, weight, ((1,), (1,)))
        input_grad = base_grad.astype(bf)
        routed, layer_out, input_grad = lax.optimization_barrier((routed, layer_out, input_grad))

        x_rows, cot_rows = routed[:, :feat], routed[:, feat:]
        own_part = jnp.concatenate(
            [
                dot(x_rows, both16[:, :feat], ((1,), (1,))),
                adapter_scale * dot(cot_rows, both16[:, feat:], ((1,), (1,))),
            ],
            axis=1,
        )
        own = own_part
        for shift in range(1, n_tensor):
            own = own + lax.ppermute(own_part, "tensor", ring(shift))
        own16 = own.astype(bf)
        down_gradient = dot(own16[:, rank:], x_rows, ((0,), (0,)))
        up_gradient = adapter_scale * dot(own16[:, :rank], cot_rows, ((0,), (0,)))

        fresh_down = optimizer_update(
            adapter_down_matrix[0], down_first_moment[0], down_second_moment[0], down_gradient
        )
        fresh_up = optimizer_update(
            adapter_up_matrix[0], up_first_moment[0], up_second_moment[0], up_gradient
        )
        return (layer_out, input_grad) + tuple(x[None] for x in fresh_down + fresh_up)

    return per_device


def solution(mesh):
    placed = (
        P("dp", "tensor"),
        P("dp", "tensor"),
        P(None, "tensor"),
        P("dp", None),
        P(),
        P("dp", None, "tensor"),
        P("dp", None, "tensor"),
        P("dp", None, "tensor"),
        P("dp", None, "tensor"),
        P("dp", None, "tensor"),
        P("dp", None, "tensor"),
    )
    return jax.shard_map(
        make(mesh.shape["dp"], mesh.shape["tensor"]),
        mesh=mesh,
        in_specs=placed,
        out_specs=(
            P("dp", "tensor"),
            P("dp", "tensor"),
            P("dp", None, "tensor"),
            P("dp", None, "tensor"),
            P("dp", None, "tensor"),
            P("dp", None, "tensor"),
            P("dp", None, "tensor"),
            P("dp", None, "tensor"),
        ),
        check_vma=False,
    )
```

```python
import jax
import jax.numpy as jnp
from jax import lax
from jax.sharding import PartitionSpec as P

adapter_scale = 2.0
learn_rate = 0.01
beta_one = 0.9
beta_two = 0.999
adam_eps = 1e-08
adam_step = 10


def optimizer_update(weight, moment, second, grad):
    moment_new = beta_one * moment + (1.0 - beta_one) * grad
    second_new = beta_two * second + (1.0 - beta_two) * grad * grad
    first_fix = 1.0 - beta_one**adam_step
    second_fix = 1.0 - beta_two**adam_step
    weight_new = weight - learn_rate * (moment_new / first_fix) / (
        jnp.sqrt(second_new / second_fix) + adam_eps
    )
    return (weight_new, moment_new, second_new)


def owner_masks(counts_row, holders, rows, rank):
    n_owner = holders.shape[0]
    order = jnp.arange(n_owner, dtype=jnp.int32)
    upper = jnp.sum(jnp.where(order[None, :] <= order[:, None], counts_row[None, :], 0), axis=1)
    lower = upper - counts_row
    select = holders[None, :] == jnp.arange(n_owner, dtype=jnp.int32)[:, None]
    start = jnp.sum(jnp.where(select, lower[None, :], 0), axis=1)
    stop = jnp.sum(jnp.where(select, upper[None, :], 0), axis=1)
    capacity = 3 * rows // (2 * n_owner)
    token = jnp.arange(rows, dtype=jnp.int32)
    slot_token = (start[:, None] + jnp.arange(capacity, dtype=jnp.int32)[None, :]).reshape(-1)
    slot_stop = jnp.repeat(stop, capacity)
    slots = (token[None, :] == slot_token[:, None]) & (token[None, :] < slot_stop[:, None])
    start = jnp.repeat(start, rank)
    stop = jnp.repeat(stop, rank)
    mask = (token[:, None] >= start[None, :]) & (token[:, None] < stop[None, :])
    return mask, slots


def fold(masked, width):
    total = masked[:, :width]
    for k in range(1, masked.shape[1] // width):
        total = total + masked[:, k * width : (k + 1) * width]
    return total


def dot(a, b, contract):
    return lax.dot_general(a, b, (contract, ((), ())), preferred_element_type=jnp.float32)


def make(n_dp, n_tensor):
    def ring(shift):
        return [(i, (i + shift) % n_tensor) for i in range(n_tensor)]

    swap_core = [(i, i ^ 1) for i in range(n_dp)]

    def per_device(
        tokens,
        cotangent,
        frozen_key_weight,
        counts,
        holder_assignment,
        adapter_down_matrix,
        adapter_up_matrix,
        down_first_moment,
        down_second_moment,
        up_first_moment,
        up_second_moment,
    ):
        rows, feat = tokens.shape
        keys = cotangent.shape[1]
        rank = adapter_down_matrix.shape[1]
        n_owner = holder_assignment.shape[0]
        width = 2 * rank
        half = feat // 2
        mine = lax.axis_index("tensor")
        core = lax.axis_index("dp") % 2
        bf = jnp.bfloat16

        mask, slots = owner_masks(counts[0], holder_assignment, rows, rank)
        pick = slots.astype(bf)
        send = jnp.concatenate(
            [dot(pick, x, ((1,), (0,))).astype(bf) for x in (tokens, cotangent)], axis=1
        )
        routed = lax.all_to_all(
            send.reshape(n_owner, -1, feat + keys), "dp", split_axis=0, concat_axis=0, tiled=True
        ).reshape(-1, feat + keys)
        both16 = jnp.concatenate(
            [adapter_down_matrix[0].astype(bf), adapter_up_matrix[0].astype(bf)], axis=1
        )
        all16 = lax.all_gather(both16, "dp", axis=0, tiled=True)

        weight_mine = lax.dynamic_slice_in_dim(frozen_key_weight, mine * feat, feat, 0)
        cots, weights = [cotangent], [weight_mine]
        for shift in range(1, n_tensor):
            cots.append(lax.ppermute(cotangent, "tensor", ring(shift)))
            target = lax.rem(mine + shift, n_tensor)
            got = lax.ppermute(
                lax.dynamic_slice_in_dim(frozen_key_weight, target * feat + core * half, half, 0),
                "tensor",
                ring(shift),
            )
            got_peer = lax.ppermute(got, "dp", swap_core)
            weights.append(
                jnp.concatenate(
                    [jnp.where(core == 0, got, got_peer), jnp.where(core == 0, got_peer, got)],
                    axis=0,
                )
            )

        base_out = dot(tokens, weight_mine, ((1,), (0,)))
        for shift in range(1, n_tensor):
            base_out = base_out + lax.ppermute(
                dot(tokens, weights[shift], ((1,), (0,))), "tensor", ring(-shift)
            )

        all16, base_out = lax.optimization_barrier((all16, base_out))
        down_all = all16[:, :feat]
        up_all = all16[:, feat:]
        hidden_part = fold(jnp.where(mask, dot(tokens, down_all, ((1,), (1,))), 0.0), width)
        back_part = fold(jnp.where(mask, dot(cotangent, up_all, ((1,), (1,))), 0.0), width)
        part = jnp.concatenate([hidden_part, adapter_scale * back_part], axis=1)
        summed = part
        for shift in range(1, n_tensor):
            summed = summed + lax.ppermute(part, "tensor", ring(shift))
        times = n_owner * rank // width
        zero = jnp.zeros((), bf)
        hidden16 = jnp.where(mask, jnp.tile(summed[:, :width].astype(bf), (1, times)), zero)
        back16 = jnp.where(mask, jnp.tile(summed[:, width:].astype(bf), (1, times)), zero)

        routed, hidden16, back16 = lax.optimization_barrier((routed, hidden16, back16))
        x_rows, cot_rows = routed[:, :feat], routed[:, feat:]
        own_part = jnp.concatenate(
            [
                dot(x_rows, both16[:, :feat], ((1,), (1,))),
                adapter_scale * dot(cot_rows, both16[:, feat:], ((1,), (1,))),
            ],
            axis=1,
        )
        own = own_part
        for shift in range(1, n_tensor):
            own = own + lax.ppermute(own_part, "tensor", ring(shift))
        own16 = own.astype(bf)
        down_gradient = dot(own16[:, rank:], x_rows, ((0,), (0,)))
        up_gradient = adapter_scale * dot(own16[:, :rank], cot_rows, ((0,), (0,)))

        layer_out = (
            base_out + adapter_scale * dot(hidden16, up_all, ((1,), (0,)))
        ).astype(bf)
        base_grad = dot(back16, down_all, ((1,), (0,)))
        for cot, weight in zip(cots, weights):
            base_grad = base_grad + dot(cot, weight, ((1,), (1,)))
        input_grad = base_grad.astype(bf)
        fresh_down = optimizer_update(
            adapter_down_matrix[0], down_first_moment[0], down_second_moment[0], down_gradient
        )
        fresh_up = optimizer_update(
            adapter_up_matrix[0], up_first_moment[0], up_second_moment[0], up_gradient
        )
        return (layer_out, input_grad) + tuple(x[None] for x in fresh_down + fresh_up)

    return per_device


def solution(mesh):
    placed = (
        P("dp", "tensor"),
        P("dp", "tensor"),
        P(None, "tensor"),
        P("dp", None),
        P(),
        P("dp", None, "tensor"),
        P("dp", None, "tensor"),
        P("dp", None, "tensor"),
        P("dp", None, "tensor"),
        P("dp", None, "tensor"),
        P("dp", None, "tensor"),
    )
    return jax.shard_map(
        make(mesh.shape["dp"], mesh.shape["tensor"]),
        mesh=mesh,
        in_specs=placed,
        out_specs=(
            P("dp", "tensor"),
            P("dp", "tensor"),
            P("dp", None, "tensor"),
            P("dp", None, "tensor"),
            P("dp", None, "tensor"),
            P("dp", None, "tensor"),
            P("dp", None, "tensor"),
            P("dp", None, "tensor"),
        ),
        check_vma=False,
    )
```
